32 devices in a mesh: lat: 4 (over y, x), lon: 8 (over z, core).
Axes of the slice: x: 2, y: 2, z: 4, core: 2. Of those that a mesh axis runs over, the one named last changes fastest.
Arguments:
- probes: float32 [8, 4, 512, 512], P(None, None, 'lon', 'lat'), may hold values from -6 to 6
- wind: float32 [2, 4, 512, 512], P(None, None, 'lon', 'lat'), may hold values from -0.45 to 0.45
- wind_tend: float32 [2, 4, 512, 512], P(None, None, 'lon', 'lat'), may hold values from -0.05 to 0.05
- obs_weight: float32 [4, 512, 512], P(None, 'lon', 'lat'), may hold values from 0.5 to 18
Outputs:
- basis: float32 [8, 4, 512, 512], P(None, None, 'lon', 'lat')
- factor: float32 [8, 8], replicated
The draws below stay inside these ranges and needn't reach their ends.
All inputs are finite; a program needn't handle non-finite values.
Results may differ from the reference program's by a relative error of at most 0.00012.
Values sent between devices are 32-bit elements; how exact they have to be, the bound alone decides.
A program may use at most 64 MiB of HBM per device.

```python
import math
import jax
import jax.numpy as jnp
from jax import lax

PROBES = 8
STEPS = 4
LEV = 4
NLON = 512
NLAT = 512
NCELLS = 1048576


def draw_obs_weight(key, part):
    noise = jax.random.uniform(key, (LEV, NLON, NLAT), jnp.float32)
    scale = jnp.exp(math.log(0.5) + noise * (math.log(2.0) - math.log(0.5)))
    lon_ramp = 1.0 + 2.0 * jnp.arange(NLON, dtype=jnp.float32) / NLON
    lat_ramp = 1.0 + 2.0 * jnp.arange(NLAT, dtype=jnp.float32) / NLAT
    return scale * lon_ramp[:, None] * lat_ramp[None, :]


def draw_wind(key, part):
    key_east = jax.random.fold_in(key, 11)
    key_north = jax.random.fold_in(key, 12)
    key_size = jax.random.fold_in(key, 13)
    lon_cells = jnp.arange(NLON, dtype=jnp.int32)
    lat_cells = jnp.arange(NLAT, dtype=jnp.int32)
    east_phase = jax.random.randint(key_east, (LEV, 1, NLAT), 0, 8)
    north_phase = jax.random.randint(key_north, (LEV, NLON, 1), 0, 8)
    east_sign = jnp.where((lon_cells[None, :, None] + east_phase) % 8 < 4, 1.0, -1.0)
    north_sign = jnp.where((lat_cells[None, None, :] + north_phase) % 8 < 4, 1.0, -1.0)
    signs = jnp.stack((east_sign, north_sign)).astype(jnp.float32)
    noise = jax.random.uniform(key_size, (2, LEV, NLON, NLAT), jnp.float32)
    size = 0.25 + 0.2 * noise
    return signs * size


def level_of(key, dims, cuts, smallest, high):
    factor_of, own = 1.0, jax.random.fold_in(key, 6)
    for dim, blocks in cuts:
        heights = jnp.exp(jax.random.uniform(jax.random.fold_in(own, dim), (blocks,), jnp.float32, smallest / len(cuts), high / len(cuts)))
        factor_of = factor_of * jnp.repeat(heights, dims[dim] // blocks).reshape([-1 if axis == dim else 1 for axis in range(len(dims))])
    return factor_of


def normal_values(stream_key, shape, scale, most, pieces=(), kind=jnp.bfloat16):
    array = jax.random.normal(stream_key, shape, jnp.float32) * scale
    if len(pieces) > 0:
        array = level_of(stream_key, shape, pieces, -0.22, 0.18) * array
    return jnp.clip(array, min=-most, max=most).astype(kind)


def setup_inputs(seed: int = 0) -> dict:
    key_list = jax.random.split(jax.random.key(seed), 5)
    return {
        "probes": normal_values(key_list[0], (PROBES, LEV, NLON, NLAT), 1.0, 6.0, ((2, 8), (3, 4)), jnp.float32),
        "wind": draw_wind(jax.random.fold_in(key_list[4], 71), 0),
        "wind_tend": jnp.clip(jax.random.uniform(key_list[2], (2, LEV, NLON, NLAT), jnp.float32, -0.05, 0.05) * level_of(key_list[2], (2, LEV, NLON, NLAT), ((2, 8), (3, 4)), -0.4, 0.0), -0.05, 0.05),
        "obs_weight": draw_obs_weight(jax.random.fold_in(key_list[4], 71), 0),
    }


diffuse = 0.24

def pad_grid(field):
    wrapped = jnp.concatenate((field[..., -1:, :], field, field[..., :1, :]), axis=-2)
    widths = ((0, 0),) * (field.ndim - 2) + ((0, 0), (1, 1))
    return jnp.pad(wrapped, widths)

def forward_step(field, lon_rate, lat_rate):
    east = lon_rate[..., 1:-1, 1:-1]
    north = lat_rate[..., 1:-1, 1:-1]
    middle = field[..., 1:-1, 1:-1]
    return (1.0 - 4.0 * diffuse) * middle + (diffuse - east) * field[..., 2:, 1:-1] + (diffuse + east) * field[..., :-2, 1:-1] + (diffuse - north) * field[..., 1:-1, 2:] + (diffuse + north) * field[..., 1:-1, :-2]

def adjoint_step(field, lon_rate, lat_rate):
    middle = field[..., 1:-1, 1:-1]
    return (1.0 - 4.0 * diffuse) * middle + (diffuse - lon_rate[..., :-2, 1:-1]) * field[..., :-2, 1:-1] + (diffuse + lon_rate[..., 2:, 1:-1]) * field[..., 2:, 1:-1] + (diffuse - lat_rate[..., 1:-1, :-2]) * field[..., 1:-1, :-2] + (diffuse + lat_rate[..., 1:-1, 2:]) * field[..., 1:-1, 2:]

def lower_inverse(lower):
    eye = jnp.eye(lower.shape[0], dtype=lower.dtype)
    return lax.linalg.triangular_solve(lower, eye, left_side=True, lower=True)

def reference(probes, wind, wind_tend, obs_weight):
    rates = []
    for step in range(STEPS):
        lon_rate = pad_grid(0.5 * (wind[0] + step * wind_tend[0]))
        lat_rate = pad_grid(0.5 * (wind[1] + step * wind_tend[1]))
        rates.append((lon_rate, lat_rate))

    def one_probe(field):
        for step in range(STEPS):
            field = forward_step(pad_grid(field), rates[step][0], rates[step][1])
        field = field * obs_weight
        for step in reversed(range(STEPS)):
            field = adjoint_step(pad_grid(field), rates[step][0], rates[step][1])
        return field
    hessian = lax.map(one_probe, probes)
    high = lax.Precision.HIGHEST
    gram = jnp.einsum('pabc,qabc->pq', hessian, hessian, precision=high)
    lower = jnp.linalg.cholesky(gram)
    result = jnp.einsum('pq,qabc->pabc', lower_inverse(lower), hessian, precision=high)
    upper = lower.T
    scale = jnp.sqrt(jnp.asarray(NCELLS, dtype=gram.dtype))
    return (result * scale, upper / scale)
```

```python
import functools
import jax
import jax.numpy as jnp
from jax import lax
from jax.experimental import pallas as pl
from jax.experimental.pallas import tpu as pltpu
from jax.sharding import PartitionSpec as P

STEPS = 4
DIFFUSE = 0.24
CENTRE = 1.0 - 4.0 * DIFFUSE
MESH = pl.DeviceIdType.MESH

HALO = 2 * STEPS
OWN = 2 * HALO
WINDOW = 32


def window_shift(side, level, width):
    if side == 0:
        return (WINDOW * level + HALO) % width
    return (WINDOW * level - (width - WINDOW + HALO)) % width


def transport_kernel(
    n_lat, n_lon, probes, wind, tend, weight, z_out, tile_out,
    field, other, masks, z_buf, send_pack, recv_pack, sums, part,
    load_sem, z_sem, lon_send, lon_recv, lat_send, lat_recv,
    sum_send, sum_recv, part_send, part_recv,
):
    count, levels, rows, width = probes.shape
    entities = count + 5
    lat = lax.axis_index("lat")
    lon = lax.axis_index("lon")
    up_lon, down_lon = lax.rem(lon + 1, n_lon), lax.rem(lon + n_lon - 1, n_lon)
    up_lat, down_lat = lax.rem(lat + 1, n_lat), lax.rem(lat + n_lat - 1, n_lat)
    lane = lax.broadcasted_iota(jnp.int32, (8, width), 1)
    row = lax.broadcasted_iota(jnp.int32, (8, width), 0)
    in_window = lane % WINDOW

    barrier = pltpu.get_barrier_semaphore()

    def greet(to_lat, to_lon):
        pl.semaphore_signal(barrier, inc=1, device_id=(to_lat, to_lon), device_id_type=MESH)

    for k in range(1, n_lon):
        greet(lat, lax.rem(lon + k, n_lon))
    for k in range(1, n_lat):
        greet(lax.rem(lat + k, n_lat), lon)
    for to_lat in (up_lat, down_lat):
        for to_lon in (up_lon, down_lon):
            greet(to_lat, to_lon)

    placed = ((probes, 0, count), (wind, count, 2), (tend, count + 2, 2), (weight, count + 4, 1))
    loads = [
        pltpu.make_async_copy(
            source,
            field.at[pl.ds(first, size), pl.ds(0, levels), pl.ds(OWN, rows), :],
            load_sem.at[k],
        )
        for k, (source, first, size) in enumerate(placed)
    ]
    for load in loads:
        load.start()

    zero = jnp.zeros((8, width), jnp.float32)
    for buffer, size in ((field, entities), (other, count)):
        for start in (0, OWN + rows + HALO):
            buffer[:, :, pl.ds(start, 8), :] = jnp.zeros((size, levels + 2, 8, width), jnp.float32)
    total = width * n_lat
    for level in range(levels):
        masks[level] = jnp.ones((8, width), jnp.float32)
    for side, first in ((0, -HALO), (1, width - WINDOW + HALO)):
        column = lat * width + first + in_window
        masks[levels + side] = jnp.where((column >= 0) & (column < total), 1.0, 0.0)

    pl.semaphore_wait(barrier, n_lon + n_lat + 2)

    lon_copies = []
    for d, (to_lon, src_row, dst_row) in enumerate(
        ((up_lon, rows - HALO, HALO), (down_lon, 0, OWN + rows))
    ):
        for k, (source, first, size) in enumerate(placed):
            copy = pltpu.make_async_remote_copy(
                src_ref=source.at[:, :, pl.ds(src_row, HALO), :],
                dst_ref=field.at[pl.ds(first, size), pl.ds(0, levels), pl.ds(dst_row, HALO), :],
                send_sem=lon_send.at[d, k],
                recv_sem=lon_recv.at[d, k],
                device_id=(lat, to_lon),
                device_id_type=MESH,
            )
            copy.start()
            lon_copies.append(copy)

    def own_window(entity, side, start):
        made = None
        for level in range(levels):
            piece = pltpu.roll(
                field[entity, level, pl.ds(start, 8), :], window_shift(side, level, width), 1
            )
            made = piece if made is None else jnp.where(lane >= WINDOW * level, piece, made)
        return made

    for load in loads:
        load.wait()

    def pack(group, carry):
        start = pl.multiple_of(OWN + 8 * group, 8)
        to = pl.multiple_of(8 * group, 8)
        for side in range(2):
            packed = [zero] * ((entities + 3) // 4)
            for entity in range(entities):
                made = own_window(entity, side, start)
                field[entity, levels + side, pl.ds(start, 8), :] = made
                slot = entity % 4
                moved = pltpu.roll(made, (8 * slot - (8 if side == 0 else 16)) % width, 1)
                packed[entity // 4] = jnp.where(
                    in_window // 8 == slot, moved, packed[entity // 4]
                )
            for k, value in enumerate(packed):
                send_pack[side, k, pl.ds(to, 8), :] = value
        return carry

    lax.fori_loop(0, rows // 8, pack, 0)

    has = (lat > 0, lat < n_lat - 1)
    lat_copies = ([], [])
    for side, to_lat in ((0, down_lat), (1, up_lat)):
        for k, (to_lon, src_row, size, dst_row) in enumerate(
            (
                (lon, 0, rows, HALO),
                (up_lon, rows - HALO, HALO, 0),
                (down_lon, 0, HALO, HALO + rows),
            )
        ):
            lat_copies[side].append(
                pltpu.make_async_remote_copy(
                    src_ref=send_pack.at[side, :, pl.ds(src_row, size), :],
                    dst_ref=recv_pack.at[1 - side, :, pl.ds(dst_row, size), :],
                    send_sem=lat_send.at[side, k],
                    recv_sem=lat_recv.at[side, k],
                    device_id=(to_lat, to_lon),
                    device_id_type=MESH,
                )
            )

    for side in range(2):
        @pl.when(has[side])
        def _():
            for copy in lat_copies[side]:
                copy.start()

    for copy in lon_copies:
        copy.wait_recv()

    for start in (HALO, OWN + rows):
        for entity in range(entities):
            for side in range(2):
                field[entity, levels + side, pl.ds(start, 8), :] = own_window(entity, side, start)

    for side in range(2):
        @pl.when(has[side])
        def _():
            for copy in lat_copies[1 - side]:
                copy.wait_recv()

        @pl.when(jnp.logical_not(has[side]))
        def _():
            recv_pack[side] = jnp.zeros(recv_pack.shape[1:], jnp.float32)

    def unpack(group, carry):
        start = pl.multiple_of(HALO + 8 * group, 8)
        at = pl.multiple_of(8 * group, 8)
        for side in range(2):
            here = in_window < 8 if side == 0 else in_window >= 24
            for entity in range(entities):
                slot = entity % 4
                got = recv_pack[side, entity // 4, pl.ds(at, 8), :]
                moved = pltpu.roll(got, ((0 if side == 0 else 24) - 8 * slot) % width, 1)
                held = field[entity, levels + side, pl.ds(start, 8), :]
                field[entity, levels + side, pl.ds(start, 8), :] = jnp.where(here, moved, held)
        return carry

    groups = rows // 8 + 2
    lax.fori_loop(0, groups, unpack, 0)

    def rate(which, step, level, start):
        now = field[count + which, level, pl.ds(start, 8), :]
        if step:
            now = now + step * field[count + 2 + which, level, pl.ds(start, 8), :]
        return 0.5 * now

    def run_step(source, target, step, adjoint):
        def body(index, carry):
            level = index // groups
            start = pl.multiple_of(HALO + 8 * (index % groups), 8)
            mask = masks[level]
            if adjoint:
                north = rate(1, step, level, start)
                before = mask * (DIFFUSE - rate(0, step, level, start - 1))
                after = mask * (DIFFUSE + rate(0, step, level, start + 1))
                left = mask * pltpu.roll(DIFFUSE - north, 1, 1)
                right = mask * pltpu.roll(DIFFUSE + north, width - 1, 1)
            else:
                if step == STEPS - 1:
                    mask = mask * field[count + 4, level, pl.ds(start, 8), :]
                east = rate(0, step, level, start)
                north = rate(1, step, level, start)
                after = mask * (DIFFUSE - east)
                before = mask * (DIFFUSE + east)
                right = mask * (DIFFUSE - north)
                left = mask * (DIFFUSE + north)
            centre = CENTRE * mask
            for probe in range(count):
                middle = source[probe, level, pl.ds(start, 8), :]
                target[probe, level, pl.ds(start, 8), :] = (
                    (centre * middle + after * source[probe, level, pl.ds(start + 1, 8), :])
                    + (before * source[probe, level, pl.ds(start - 1, 8), :]
                       + right * pltpu.roll(middle, width - 1, 1))
                    + left * pltpu.roll(middle, 1, 1)
                )
            return carry

        lax.fori_loop(0, (levels + 2) * groups, body, 0)

    source, target = field, other
    for step in range(STEPS):
        run_step(source, target, step, False)
        source, target = target, source
    for step in reversed(range(STEPS)):
        run_step(source, target, step, True)
        source, target = target, source

    pairs = [(p, q) for p in range(count) for q in range(p, count)]

    accs = [zero] * len(pairs)
    for level in range(levels):
        def gather(group, accs):
            start = pl.multiple_of(OWN + 8 * group, 8)
            to = pl.multiple_of(8 * group, 8)
            values = []
            for probe in range(count):
                first = pltpu.roll(
                    source[probe, levels, pl.ds(start, 8), :],
                    (width - window_shift(0, level, width)) % width, 1,
                )
                last = pltpu.roll(
                    source[probe, levels + 1, pl.ds(start, 8), :],
                    (width - window_shift(1, level, width)) % width, 1,
                )
                value = source[probe, level, pl.ds(start, 8), :]
                value = jnp.where(lane < HALO, first, value)
                value = jnp.where(lane >= width - HALO, last, value)
                z_buf[probe, level, pl.ds(to, 8), :] = value
                values.append(value)
            return tuple(a + values[p] * values[q] for a, (p, q) in zip(accs, pairs))

        accs = lax.fori_loop(0, rows // 8, gather, tuple(accs))

    z_copy = pltpu.make_async_copy(z_buf, z_out, z_sem)
    z_copy.start()

    reduced = {
        pair: jnp.broadcast_to(jnp.sum(acc, axis=0, keepdims=True), (8, width))
        for pair, acc in zip(pairs, accs)
    }
    gram = zero
    for q in range(count):
        column = zero
        for p in range(count):
            column = jnp.where(row == p, reduced[(min(p, q), max(p, q))], column)
        gram = jnp.where(lane == q, jnp.sum(column, axis=1, keepdims=True), gram)

    def all_sum(value, slots, size, me, peer, send, recv):
        slots[me] = value
        copies = []
        for k in range(1, size):
            copy = pltpu.make_async_remote_copy(
                src_ref=slots.at[me],
                dst_ref=slots.at[me],
                send_sem=send.at[k],
                recv_sem=recv.at[k],
                device_id=peer(lax.rem(me + k, size)),
                device_id_type=MESH,
            )
            copy.start()
            copies.append(copy)
        for k, copy in enumerate(copies):
            came = lax.rem(me + size - (k + 1), size)
            pltpu.make_async_remote_copy(
                src_ref=slots.at[came],
                dst_ref=slots.at[came],
                send_sem=send.at[k + 1],
                recv_sem=recv.at[k + 1],
                device_id=peer(lax.rem(me + k + 1, size)),
                device_id_type=MESH,
            ).wait_recv()
        out = slots[0]
        for k in range(1, size):
            out = out + slots[k]
        return out, copies

    gram, first_copies = all_sum(gram, sums, n_lon, lon, lambda i: (lat, i), sum_send, sum_recv)
    gram, last_copies = all_sum(gram, part, n_lat, lat, lambda i: (i, lon), part_send, part_recv)

    work = jnp.where(lane == row + count, 1.0, jnp.where(lane < count, gram, 0.0))
    result = zero
    for k in range(count):
        pivot = work[k : k + 1, :]
        diagonal = pivot[:, k : k + 1]
        pivot = pivot * (1.0 / jnp.sqrt(diagonal))
        result = jnp.where((row == k) & (lane >= k), pivot, result)
        work = work - jnp.where(row > k, (work[:, k : k + 1] * (1.0 / diagonal)), 0.0) * work[k : k + 1, :]
    tile_out[...] = result

    for copy in first_copies + last_copies:
        copy.wait_send()
    for copy in lon_copies:
        copy.wait_send()
    for side in range(2):
        @pl.when(has[side])
        def _():
            for copy in lat_copies[side]:
                copy.wait_send()
    z_copy.wait()


def apply_kernel(scale, inverse, tile, z, basis, factor):
    count, _, rows, width = z.shape
    coefficients = [
        [inverse[p, count + q] * scale for q in range(p + 1)] for p in range(count)
    ]
    for start in range(0, rows, 8):
        values = [z[q, 0, pl.ds(start, 8), :] for q in range(count)]
        for p in range(count):
            total = coefficients[p][0] * values[0]
            for q in range(1, p + 1):
                total = total + coefficients[p][q] * values[q]
            basis[p, 0, pl.ds(start, 8), :] = total

    @pl.when(pl.program_id(0) == 0)
    def _():
        factor[...] = tile[:, :count] * (1.0 / scale)


def body(probes, wind, wind_tend, obs_weight, *, n_lat, n_lon):
    count, levels, rows, width = probes.shape
    entities = count + 5
    packs = (entities + 3) // 4
    tall = rows + 4 * HALO
    f32 = jnp.float32
    z, tile = pl.pallas_call(
        functools.partial(transport_kernel, n_lat, n_lon),
        out_shape=(
            jax.ShapeDtypeStruct(probes.shape, f32),
            jax.ShapeDtypeStruct((8, width), f32),
        ),
        in_specs=[pl.BlockSpec(memory_space=pl.ANY)] * 4,
        out_specs=(
            pl.BlockSpec(memory_space=pl.ANY),
            pl.BlockSpec(memory_space=pltpu.VMEM),
        ),
        scratch_shapes=[
            pltpu.VMEM((entities, levels + 2, tall, width), f32),
            pltpu.VMEM((count, levels + 2, tall, width), f32),
            pltpu.VMEM((levels + 2, 8, width), f32),
            pltpu.VMEM(probes.shape, f32),
            pltpu.VMEM((2, packs, rows, width), f32),
            pltpu.VMEM((2, packs, rows + 2 * HALO, width), f32),
            pltpu.VMEM((n_lon, 8, width), f32),
            pltpu.VMEM((n_lat, 8, width), f32),
            pltpu.SemaphoreType.DMA((4,)),
            pltpu.SemaphoreType.DMA,
            pltpu.SemaphoreType.DMA((2, 4)),
            pltpu.SemaphoreType.DMA((2, 4)),
            pltpu.SemaphoreType.DMA((2, 3)),
            pltpu.SemaphoreType.DMA((2, 3)),
            pltpu.SemaphoreType.DMA((n_lon,)),
            pltpu.SemaphoreType.DMA((n_lon,)),
            pltpu.SemaphoreType.DMA((n_lat,)),
            pltpu.SemaphoreType.DMA((n_lat,)),
        ],
        compiler_params=pltpu.CompilerParams(
            collective_id=0, has_side_effects=True, vmem_limit_bytes=32 * 2**20
        ),
        name="transport",
    )(probes, wind, wind_tend, obs_weight[None])

    cells = levels * rows * width * n_lat * n_lon
    block = pl.BlockSpec((count, 1, rows, width), lambda level: (0, level, 0, 0))
    basis, factor = pl.pallas_call(
        functools.partial(apply_kernel, float(cells) ** 0.5),
        grid=(levels,),
        out_shape=(
            jax.ShapeDtypeStruct(probes.shape, f32),
            jax.ShapeDtypeStruct((count, count), f32),
        ),
        in_specs=[
            pl.BlockSpec(memory_space=pltpu.SMEM),
            pl.BlockSpec((8, width), lambda level: (0, 0)),
            block,
        ],
        out_specs=(block, pl.BlockSpec((count, count), lambda level: (0, 0))),
        compiler_params=pltpu.CompilerParams(vmem_limit_bytes=16 * 2**20),
        name="orthonormal",
    )(tile, tile, z)
    return basis, factor


def solution(mesh):
    placed = (
        P(None, None, "lon", "lat"),
        P(None, None, "lon", "lat"),
        P(None, None, "lon", "lat"),
        P(None, "lon", "lat"),
    )
    return jax.shard_map(
        functools.partial(body, n_lat=mesh.shape["lat"], n_lon=mesh.shape["lon"]),
        mesh=mesh,
        in_specs=placed,
        out_specs=(P(None, None, "lon", "lat"), P()),
        check_vma=False,
    )
```

```python
import functools
import jax
import jax.numpy as jnp
from jax import lax
from jax.experimental import pallas as pl
from jax.experimental.pallas import tpu as pltpu
from jax.sharding import PartitionSpec as P

STEPS = 4
DIFFUSE = 0.24
CENTRE = 1.0 - 4.0 * DIFFUSE
MESH = pl.DeviceIdType.MESH

HALO = 2 * STEPS
OWN = 2 * HALO
WINDOW = 32


def window_shift(side, level, width):
    if side == 0:
        return (WINDOW * level + HALO) % width
    return (WINDOW * level - (width - WINDOW + HALO)) % width


def transport_kernel(
    n_lat, n_lon, probes, wind, tend, weight, z_out, tile_out,
    field, other, masks, z_buf, send_pack, recv_pack, sums, part,
    load_sem, z_sem, lon_send, lon_recv, lat_send, lat_recv,
    sum_send, sum_recv, part_send, part_recv,
):
    count, levels, rows, width = probes.shape
    entities = count + 5
    lat = lax.axis_index("lat")
    lon = lax.axis_index("lon")
    up_lon, down_lon = lax.rem(lon + 1, n_lon), lax.rem(lon + n_lon - 1, n_lon)
    up_lat, down_lat = lax.rem(lat + 1, n_lat), lax.rem(lat + n_lat - 1, n_lat)
    lane = lax.broadcasted_iota(jnp.int32, (8, width), 1)
    row = lax.broadcasted_iota(jnp.int32, (8, width), 0)
    in_window = lane % WINDOW

    barrier = pltpu.get_barrier_semaphore()

    def greet(to_lat, to_lon):
        pl.semaphore_signal(barrier, inc=1, device_id=(to_lat, to_lon), device_id_type=MESH)

    for k in range(1, n_lon):
        greet(lat, lax.rem(lon + k, n_lon))
    for k in range(1, n_lat):
        greet(lax.rem(lat + k, n_lat), lon)
    for to_lat in (up_lat, down_lat):
        for to_lon in (up_lon, down_lon):
            greet(to_lat, to_lon)

    placed = ((probes, 0, count), (wind, count, 2), (tend, count + 2, 2), (weight, count + 4, 1))
    loads = [
        pltpu.make_async_copy(
            source,
            field.at[pl.ds(first, size), pl.ds(0, levels), pl.ds(OWN, rows), :],
            load_sem.at[k],
        )
        for k, (source, first, size) in enumerate(placed)
    ]
    for load in loads:
        load.start()

    zero = jnp.zeros((8, width), jnp.float32)
    for buffer, size in ((field, entities), (other, count)):
        for start in (0, OWN + rows + HALO):
            buffer[:, :, pl.ds(start, 8), :] = jnp.zeros((size, levels + 2, 8, width), jnp.float32)
    total = width * n_lat
    for level in range(levels):
        masks[level] = jnp.ones((8, width), jnp.float32)
    for side, first in ((0, -HALO), (1, width - WINDOW + HALO)):
        column = lat * width + first + in_window
        masks[levels + side] = jnp.where((column >= 0) & (column < total), 1.0, 0.0)

    pl.semaphore_wait(barrier, n_lon + n_lat + 2)

    lon_copies = []
    for d, (to_lon, src_row, dst_row) in enumerate(
        ((up_lon, rows - HALO, HALO), (down_lon, 0, OWN + rows))
    ):
        for k, (source, first, size) in enumerate(placed):
            copy = pltpu.make_async_remote_copy(
                src_ref=source.at[:, :, pl.ds(src_row, HALO), :],
                dst_ref=field.at[pl.ds(first, size), pl.ds(0, levels), pl.ds(dst_row, HALO), :],
                send_sem=lon_send.at[d, k],
                recv_sem=lon_recv.at[d, k],
                device_id=(lat, to_lon),
                device_id_type=MESH,
            )
            copy.start()
            lon_copies.append(copy)

    def own_window(entity, side, start):
        made = None
        for level in range(levels):
            piece = pltpu.roll(
                field[entity, level, pl.ds(start, 8), :], window_shift(side, level, width), 1
            )
            made = piece if made is None else jnp.where(lane >= WINDOW * level, piece, made)
        return made

    for load in loads:
        load.wait()

    def pack(group, carry):
        start = pl.multiple_of(OWN + 8 * group, 8)
        to = pl.multiple_of(8 * group, 8)
        for side in range(2):
            packed = [zero] * ((entities + 3) // 4)
            for entity in range(entities):
                made = own_window(entity, side, start)
                field[entity, levels + side, pl.ds(start, 8), :] = made
                slot = entity % 4
                moved = pltpu.roll(made, (8 * slot - (8 if side == 0 else 16)) % width, 1)
                packed[entity // 4] = jnp.where(
                    in_window // 8 == slot, moved, packed[entity // 4]
                )
            for k, value in enumerate(packed):
                send_pack[side, k, pl.ds(to, 8), :] = value
        return carry

    lax.fori_loop(0, rows // 8, pack, 0)

    has = (lat > 0, lat < n_lat - 1)
    lat_copies = ([], [])
    for side, to_lat in ((0, down_lat), (1, up_lat)):
        for k, (to_lon, src_row, size, dst_row) in enumerate(
            (
                (lon, 0, rows, HALO),
                (up_lon, rows - HALO, HALO, 0),
                (down_lon, 0, HALO, HALO + rows),
            )
        ):
            lat_copies[side].append(
                pltpu.make_async_remote_copy(
                    src_ref=send_pack.at[side, :, pl.ds(src_row, size), :],
                    dst_ref=recv_pack.at[1 - side, :, pl.ds(dst_row, size), :],
                    send_sem=lat_send.at[side, k],
                    recv_sem=lat_recv.at[side, k],
                    device_id=(to_lat, to_lon),
                    device_id_type=MESH,
                )
            )

    for side in range(2):
        @pl.when(has[side])
        def _():
            for copy in lat_copies[side]:
                copy.start()

    for copy in lon_copies:
        copy.wait_recv()

    for start in (HALO, OWN + rows):
        for entity in range(entities):
            for side in range(2):
                field[entity, levels + side, pl.ds(start, 8), :] = own_window(entity, side, start)

    for side in range(2):
        @pl.when(has[side])
        def _():
            for copy in lat_copies[1 - side]:
                copy.wait_recv()

        @pl.when(jnp.logical_not(has[side]))
        def _():
            recv_pack[side] = jnp.zeros(recv_pack.shape[1:], jnp.float32)

    def unpack(group, carry):
        start = pl.multiple_of(HALO + 8 * group, 8)
        at = pl.multiple_of(8 * group, 8)
        for side in range(2):
            here = in_window < 8 if side == 0 else in_window >= 24
            for entity in range(entities):
                slot = entity % 4
                got = recv_pack[side, entity // 4, pl.ds(at, 8), :]
                moved = pltpu.roll(got, ((0 if side == 0 else 24) - 8 * slot) % width, 1)
                held = field[entity, levels + side, pl.ds(start, 8), :]
                field[entity, levels + side, pl.ds(start, 8), :] = jnp.where(here, moved, held)
        return carry

    groups = rows // 8 + 2
    lax.fori_loop(0, groups, unpack, 0, unroll=2)

    def rate(which, step, level, start):
        now = field[count + which, level, pl.ds(start, 8), :]
        if step:
            now = now + step * field[count + 2 + which, level, pl.ds(start, 8), :]
        return 0.5 * now

    def run_step(source, target, step, adjoint, first, last):
        def body(level, carry):
            edge = masks[level]
            for group in range(first, last):
                start = HALO + 8 * group
                mask = edge
                if adjoint:
                    north = rate(1, step, level, start)
                    before = mask * (DIFFUSE - rate(0, step, level, start - 1))
                    after = mask * (DIFFUSE + rate(0, step, level, start + 1))
                    left = mask * pltpu.roll(DIFFUSE - north, 1, 1)
                    right = mask * pltpu.roll(DIFFUSE + north, width - 1, 1)
                else:
                    if step == STEPS - 1:
                        mask = mask * field[count + 4, level, pl.ds(start, 8), :]
                    east = rate(0, step, level, start)
                    north = rate(1, step, level, start)
                    after = mask * (DIFFUSE - east)
                    before = mask * (DIFFUSE + east)
                    right = mask * (DIFFUSE - north)
                    left = mask * (DIFFUSE + north)
                centre = CENTRE * mask
                for probe in range(count):
                    middle = source[probe, level, pl.ds(start, 8), :]
                    target[probe, level, pl.ds(start, 8), :] = (
                        (centre * middle + after * source[probe, level, pl.ds(start + 1, 8), :])
                        + (before * source[probe, level, pl.ds(start - 1, 8), :]
                           + right * pltpu.roll(middle, width - 1, 1))
                        + left * pltpu.roll(middle, 1, 1)
                    )
            return carry

        lax.fori_loop(0, levels + 2, body, 0)

    source, target = field, other
    for step in range(STEPS):
        run_step(source, target, step, False, 0, groups)
        source, target = target, source
    for step in reversed(range(STEPS)):
        run_step(source, target, step, True, int(step == 0), groups - int(step == 0))
        source, target = target, source

    pairs = [(p, q) for p in range(count) for q in range(p, count)]

    accs = [zero] * len(pairs)
    for level in range(levels):
        def gather(group, accs):
            start = pl.multiple_of(OWN + 8 * group, 8)
            to = pl.multiple_of(8 * group, 8)
            values = []
            for probe in range(count):
                first = pltpu.roll(
                    source[probe, levels, pl.ds(start, 8), :],
                    (width - window_shift(0, level, width)) % width, 1,
                )
                last = pltpu.roll(
                    source[probe, levels + 1, pl.ds(start, 8), :],
                    (width - window_shift(1, level, width)) % width, 1,
                )
                value = source[probe, level, pl.ds(start, 8), :]
                value = jnp.where(lane < HALO, first, value)
                value = jnp.where(lane >= width - HALO, last, value)
                z_buf[probe, level, pl.ds(to, 8), :] = value
                values.append(value)
            return tuple(a + values[p] * values[q] for a, (p, q) in zip(accs, pairs))

        accs = lax.fori_loop(0, rows // 8, gather, tuple(accs), unroll=4)

    z_copy = pltpu.make_async_copy(z_buf, z_out, z_sem)
    z_copy.start()

    reduced = {
        pair: jnp.broadcast_to(jnp.sum(acc, axis=0, keepdims=True), (8, width))
        for pair, acc in zip(pairs, accs)
    }
    gram = zero
    for q in range(count):
        column = zero
        for p in range(count):
            column = jnp.where(row == p, reduced[(min(p, q), max(p, q))], column)
        gram = jnp.where(lane == q, jnp.sum(column, axis=1, keepdims=True), gram)

    def all_sum(value, slots, size, me, peer, send, recv):
        slots[me] = value
        copies = []
        for k in range(1, size):
            copy = pltpu.make_async_remote_copy(
                src_ref=slots.at[me],
                dst_ref=slots.at[me],
                send_sem=send.at[k],
                recv_sem=recv.at[k],
                device_id=peer(lax.rem(me + k, size)),
                device_id_type=MESH,
            )
            copy.start()
            copies.append(copy)
        for k, copy in enumerate(copies):
            came = lax.rem(me + size - (k + 1), size)
            pltpu.make_async_remote_copy(
                src_ref=slots.at[came],
                dst_ref=slots.at[came],
                send_sem=send.at[k + 1],
                recv_sem=recv.at[k + 1],
                device_id=peer(lax.rem(me + k + 1, size)),
                device_id_type=MESH,
            ).wait_recv()
        out = slots[0]
        for k in range(1, size):
            out = out + slots[k]
        return out, copies

    gram, first_copies = all_sum(gram, sums, n_lon, lon, lambda i: (lat, i), sum_send, sum_recv)
    gram, last_copies = all_sum(gram, part, n_lat, lat, lambda i: (i, lon), part_send, part_recv)

    work = jnp.where(lane == row + count, 1.0, jnp.where(lane < count, gram, 0.0))
    result = zero
    for k in range(count):
        pivot = work[k : k + 1, :]
        diagonal = pivot[:, k : k + 1]
        pivot = pivot * (1.0 / jnp.sqrt(diagonal))
        result = jnp.where((row == k) & (lane >= k), pivot, result)
        work = work - jnp.where(row > k, (work[:, k : k + 1] * (1.0 / diagonal)), 0.0) * work[k : k + 1, :]
    tile_out[...] = result

    for copy in first_copies + last_copies:
        copy.wait_send()
    for copy in lon_copies:
        copy.wait_send()
    for side in range(2):
        @pl.when(has[side])
        def _():
            for copy in lat_copies[side]:
                copy.wait_send()
    z_copy.wait()


def apply_kernel(scale, inverse, tile, z, basis, factor):
    count, _, rows, width = z.shape
    coefficients = [
        [inverse[p, count + q] * scale for q in range(p + 1)] for p in range(count)
    ]
    for start in range(0, rows, 8):
        values = [z[q, 0, pl.ds(start, 8), :] for q in range(count)]
        for p in range(count):
            total = coefficients[p][0] * values[0]
            for q in range(1, p + 1):
                total = total + coefficients[p][q] * values[q]
            basis[p, 0, pl.ds(start, 8), :] = total

    @pl.when(pl.program_id(0) == 0)
    def _():
        factor[...] = tile[:, :count] * (1.0 / scale)


def body(probes, wind, wind_tend, obs_weight, *, n_lat, n_lon):
    count, levels, rows, width = probes.shape
    entities = count + 5
    packs = (entities + 3) // 4
    tall = rows + 4 * HALO
    f32 = jnp.float32
    z, tile = pl.pallas_call(
        functools.partial(transport_kernel, n_lat, n_lon),
        out_shape=(
            jax.ShapeDtypeStruct(probes.shape, f32),
            jax.ShapeDtypeStruct((8, width), f32),
        ),
        in_specs=[pl.BlockSpec(memory_space=pltpu.HBM)] * 4,
        out_specs=(
            pl.BlockSpec(memory_space=pl.ANY),
            pl.BlockSpec(memory_space=pltpu.VMEM),
        ),
        scratch_shapes=[
            pltpu.VMEM((entities, levels + 2, tall, width), f32),
            pltpu.VMEM((count, levels + 2, tall, width), f32),
            pltpu.VMEM((levels + 2, 8, width), f32),
            pltpu.VMEM(probes.shape, f32),
            pltpu.VMEM((2, packs, rows, width), f32),
            pltpu.VMEM((2, packs, rows + 2 * HALO, width), f32),
            pltpu.VMEM((n_lon, 8, width), f32),
            pltpu.VMEM((n_lat, 8, width), f32),
            pltpu.SemaphoreType.DMA((4,)),
            pltpu.SemaphoreType.DMA,
            pltpu.SemaphoreType.DMA((2, 4)),
            pltpu.SemaphoreType.DMA((2, 4)),
            pltpu.SemaphoreType.DMA((2, 3)),
            pltpu.SemaphoreType.DMA((2, 3)),
            pltpu.SemaphoreType.DMA((n_lon,)),
            pltpu.SemaphoreType.DMA((n_lon,)),
            pltpu.SemaphoreType.DMA((n_lat,)),
            pltpu.SemaphoreType.DMA((n_lat,)),
        ],
        compiler_params=pltpu.CompilerParams(
            collective_id=0, has_side_effects=True, vmem_limit_bytes=60 * 2**20
        ),
        name="transport",
    )(probes, wind, wind_tend, obs_weight[None])

    cells = levels * rows * width * n_lat * n_lon
    block = pl.BlockSpec((count, 1, rows, width), lambda level: (0, level, 0, 0))
    basis, factor = pl.pallas_call(
        functools.partial(apply_kernel, float(cells) ** 0.5),
        grid=(levels,),
        out_shape=(
            jax.ShapeDtypeStruct(probes.shape, f32),
            jax.ShapeDtypeStruct((count, count), f32),
        ),
        in_specs=[
            pl.BlockSpec(memory_space=pltpu.SMEM),
            pl.BlockSpec((8, width), lambda level: (0, 0)),
            block,
        ],
        out_specs=(block, pl.BlockSpec((count, count), lambda level: (0, 0))),
        compiler_params=pltpu.CompilerParams(vmem_limit_bytes=60 * 2**20),
        name="orthonormal",
    )(tile, tile, z)
    return basis, factor


def solution(mesh):
    placed = (
        P(None, None, "lon", "lat"),
        P(None, None, "lon", "lat"),
        P(None, None, "lon", "lat"),
        P(None, "lon", "lat"),
    )
    return jax.shard_map(
        functools.partial(body, n_lat=mesh.shape["lat"], n_lon=mesh.shape["lon"]),
        mesh=mesh,
        in_specs=placed,
        out_specs=(P(None, None, "lon", "lat"), P()),
        check_vma=False,
    )
```

```python
import functools
import jax
import jax.numpy as jnp
from jax import lax
from jax.experimental import pallas as pl
from jax.experimental.pallas import tpu as pltpu
from jax.sharding import PartitionSpec as P

STEPS = 4
DIFFUSE = 0.24
CENTRE = 1.0 - 4.0 * DIFFUSE
MESH = pl.DeviceIdType.MESH

HALO = 2 * STEPS
WINDOW = 32


def window_shift(side, level, width):
    if side == 0:
        return (WINDOW * level + HALO) % width
    return (WINDOW * level - (width - WINDOW + HALO)) % width


def transport_kernel(
    n_lat, n_lon, probes, wind, tend, weight, z_out, tile_out,
    field, stages, masks, z_buf, send_pack, recv_pack, sums, part,
    load_sem, z_sem, lon_send, lon_recv, lat_send, lat_recv,
    sum_send, sum_recv, part_send, part_recv,
):
    count, levels, rows, width = probes.shape
    entities = count + 5
    lat = lax.axis_index("lat")
    lon = lax.axis_index("lon")
    up_lon, down_lon = lax.rem(lon + 1, n_lon), lax.rem(lon + n_lon - 1, n_lon)
    up_lat, down_lat = lax.rem(lat + 1, n_lat), lax.rem(lat + n_lat - 1, n_lat)
    lane = lax.broadcasted_iota(jnp.int32, (8, width), 1)
    row = lax.broadcasted_iota(jnp.int32, (8, width), 0)
    in_window = lane % WINDOW

    barrier = pltpu.get_barrier_semaphore()

    def greet(to_lat, to_lon):
        pl.semaphore_signal(barrier, inc=1, device_id=(to_lat, to_lon), device_id_type=MESH)

    for k in range(1, n_lon):
        greet(lat, lax.rem(lon + k, n_lon))
    for k in range(1, n_lat):
        greet(lax.rem(lat + k, n_lat), lon)
    for to_lat in (up_lat, down_lat):
        for to_lon in (up_lon, down_lon):
            greet(to_lat, to_lon)

    placed = ((probes, 0, count), (wind, count, 2), (tend, count + 2, 2), (weight, count + 4, 1))
    loads = [
        pltpu.make_async_copy(
            source,
            field.at[pl.ds(first, size), pl.ds(0, levels), pl.ds(HALO, rows), :],
            load_sem.at[k],
        )
        for k, (source, first, size) in enumerate(placed)
    ]
    for load in loads:
        load.start()

    zero = jnp.zeros((8, width), jnp.float32)
    total = width * n_lat
    for side, first in ((0, -HALO), (1, width - WINDOW + HALO)):
        column = lat * width + first + in_window
        masks[side] = jnp.where((column >= 0) & (column < total), 1.0, 0.0)

    pl.semaphore_wait(barrier, n_lon + n_lat + 2)

    lon_copies = []
    for d, (to_lon, src_row, dst_row) in enumerate(
        ((up_lon, rows - HALO, 0), (down_lon, 0, HALO + rows))
    ):
        for k, (source, first, size) in enumerate(placed):
            copy = pltpu.make_async_remote_copy(
                src_ref=source.at[:, :, pl.ds(src_row, HALO), :],
                dst_ref=field.at[pl.ds(first, size), pl.ds(0, levels), pl.ds(dst_row, HALO), :],
                send_sem=lon_send.at[d, k],
                recv_sem=lon_recv.at[d, k],
                device_id=(lat, to_lon),
                device_id_type=MESH,
            )
            copy.start()
            lon_copies.append(copy)

    def own_window(entity, side, start):
        made = None
        for level in range(levels):
            piece = pltpu.roll(
                field[entity, level, pl.ds(start, 8), :], window_shift(side, level, width), 1
            )
            made = piece if made is None else jnp.where(lane >= WINDOW * level, piece, made)
        return made

    for load in loads:
        load.wait()

    def pack(group, carry):
        start = pl.multiple_of(HALO + 8 * group, 8)
        to = pl.multiple_of(8 * group, 8)
        for side in range(2):
            packed = [zero] * ((entities + 3) // 4)
            for entity in range(entities):
                made = own_window(entity, side, start)
                field[entity, levels + side, pl.ds(start, 8), :] = made
                slot = entity % 4
                moved = pltpu.roll(made, (8 * slot - (8 if side == 0 else 16)) % width, 1)
                packed[entity // 4] = jnp.where(
                    in_window // 8 == slot, moved, packed[entity // 4]
                )
            for k, value in enumerate(packed):
                send_pack[side, k, pl.ds(to, 8), :] = value
        return carry

    lax.fori_loop(0, rows // 8, pack, 0)

    has = (lat > 0, lat < n_lat - 1)
    lat_copies = ([], [])
    for side, to_lat in ((0, down_lat), (1, up_lat)):
        for k, (to_lon, src_row, size, dst_row) in enumerate(
            (
                (lon, 0, rows, HALO),
                (up_lon, rows - HALO, HALO, 0),
                (down_lon, 0, HALO, HALO + rows),
            )
        ):
            lat_copies[side].append(
                pltpu.make_async_remote_copy(
                    src_ref=send_pack.at[side, :, pl.ds(src_row, size), :],
                    dst_ref=recv_pack.at[1 - side, :, pl.ds(dst_row, size), :],
                    send_sem=lat_send.at[side, k],
                    recv_sem=lat_recv.at[side, k],
                    device_id=(to_lat, to_lon),
                    device_id_type=MESH,
                )
            )

    for side in range(2):
        @pl.when(has[side])
        def _():
            for copy in lat_copies[side]:
                copy.start()

    groups = rows // 8 + 2
    buffers = [field] + [stages.at[k] for k in range(2 * STEPS)]

    def above(ref, lead, start, closed):
        if closed:
            return pltpu.roll(ref[(*lead, pl.ds(start, 8), slice(None))], 1, 0)
        return ref[(*lead, pl.ds(start - 1, 8), slice(None))]

    def below(ref, lead, start, closed):
        if closed:
            return pltpu.roll(ref[(*lead, pl.ds(start, 8), slice(None))], 7, 0)
        return ref[(*lead, pl.ds(start + 1, 8), slice(None))]

    def same(ref, lead, start, closed):
        return ref[(*lead, pl.ds(start, 8), slice(None))]

    def rate(which, step, level, start, read=same, closed=False):
        now = read(field, (count + which, level), start, closed)
        if step:
            now = now + step * read(field, (count + 2 + which, level), start, closed)
        return 0.5 * now

    def run_step(number, first_level, last_level, chosen, top, bottom, unroll):
        source, target = buffers[number], buffers[number + 1]
        adjoint = number >= STEPS
        step = 2 * STEPS - 1 - number if adjoint else number

        def body(level, carry):
            for group in chosen:
                start = 8 * group
                if adjoint:
                    north = rate(1, step, level, start)
                    before = DIFFUSE - rate(0, step, level, start, above, group == top)
                    after = DIFFUSE + rate(0, step, level, start, below, group == bottom)
                    left = pltpu.roll(DIFFUSE - north, 1, 1)
                    right = pltpu.roll(DIFFUSE + north, width - 1, 1)
                else:
                    east = rate(0, step, level, start)
                    north = rate(1, step, level, start)
                    after = DIFFUSE - east
                    before = DIFFUSE + east
                    right = DIFFUSE - north
                    left = DIFFUSE + north
                centre = CENTRE
                scale = None
                if first_level >= levels:
                    scale = masks[level - levels]
                if number == STEPS - 1:
                    seen = field[count + 4, level, pl.ds(start, 8), :]
                    scale = seen if scale is None else scale * seen
                if scale is not None:
                    centre, before, after, left, right = (
                        scale * x for x in (centre, before, after, left, right)
                    )
                for probe in range(count):
                    lead = (probe, level)
                    middle = source[probe, level, pl.ds(start, 8), :]
                    target[probe, level, pl.ds(start, 8), :] = (
                        (centre * middle + after * below(source, lead, start, group == bottom))
                        + (before * above(source, lead, start, group == top)
                           + right * pltpu.roll(middle, width - 1, 1))
                        + left * pltpu.roll(middle, 1, 1)
                    )
            return carry

        lax.fori_loop(first_level, last_level, body, 0, unroll=unroll)

    for number in range(2 * STEPS):
        run_step(number, 0, levels, range(1, groups - 1), 1, groups - 2, 1)

    for copy in lon_copies:
        copy.wait_recv()

    for start in (0, HALO + rows):
        for entity in range(entities):
            for side in range(2):
                field[entity, levels + side, pl.ds(start, 8), :] = own_window(entity, side, start)

    for side in range(2):
        @pl.when(has[side])
        def _():
            for copy in lat_copies[1 - side]:
                copy.wait_recv()

        @pl.when(jnp.logical_not(has[side]))
        def _():
            recv_pack[side] = jnp.zeros(recv_pack.shape[1:], jnp.float32)

    def unpack(group, carry):
        at = pl.multiple_of(8 * group, 8)
        for side in range(2):
            here = in_window < 8 if side == 0 else in_window >= 24
            for entity in range(entities):
                slot = entity % 4
                got = recv_pack[side, entity // 4, pl.ds(at, 8), :]
                moved = pltpu.roll(got, ((0 if side == 0 else 24) - 8 * slot) % width, 1)
                held = field[entity, levels + side, pl.ds(at, 8), :]
                field[entity, levels + side, pl.ds(at, 8), :] = jnp.where(here, moved, held)
        return carry

    lax.fori_loop(0, groups, unpack, 0, unroll=2)

    for number in range(2 * STEPS):
        last = int(number == 2 * STEPS - 1)
        outer = (1, groups - 2) if last else (0, 1, groups - 2, groups - 1)
        run_step(number, 0, levels, outer, 0, groups - 1, 2)
        run_step(number, levels, levels + 2, range(last, groups - last), 0, groups - 1, 1)
    source = buffers[-1]

    pairs = [(p, q) for p in range(count) for q in range(p, count)]

    accs = [zero] * len(pairs)
    for level in range(levels):
        def gather(group, accs):
            start = pl.multiple_of(HALO + 8 * group, 8)
            to = pl.multiple_of(8 * group, 8)
            values = []
            for probe in range(count):
                first = pltpu.roll(
                    source[probe, levels, pl.ds(start, 8), :],
                    (width - window_shift(0, level, width)) % width, 1,
                )
                last = pltpu.roll(
                    source[probe, levels + 1, pl.ds(start, 8), :],
                    (width - window_shift(1, level, width)) % width, 1,
                )
                value = source[probe, level, pl.ds(start, 8), :]
                value = jnp.where(lane < HALO, first, value)
                value = jnp.where(lane >= width - HALO, last, value)
                z_buf[probe, level, pl.ds(to, 8), :] = value
                values.append(value)
            return tuple(a + values[p] * values[q] for a, (p, q) in zip(accs, pairs))

        accs = lax.fori_loop(0, rows // 8, gather, tuple(accs), unroll=4)

    z_copy = pltpu.make_async_copy(z_buf, z_out, z_sem)
    z_copy.start()

    reduced = {
        pair: jnp.broadcast_to(jnp.sum(acc, axis=0, keepdims=True), (8, width))
        for pair, acc in zip(pairs, accs)
    }
    gram = zero
    for q in range(count):
        column = zero
        for p in range(count):
            column = jnp.where(row == p, reduced[(min(p, q), max(p, q))], column)
        gram = jnp.where(lane == q, jnp.sum(column, axis=1, keepdims=True), gram)

    def all_sum(value, slots, size, me, peer, send, recv):
        slots[me] = value
        copies = []
        for k in range(1, size):
            copy = pltpu.make_async_remote_copy(
                src_ref=slots.at[me],
                dst_ref=slots.at[me],
                send_sem=send.at[k],
                recv_sem=recv.at[k],
                device_id=peer(lax.rem(me + k, size)),
                device_id_type=MESH,
            )
            copy.start()
            copies.append(copy)
        for k, copy in enumerate(copies):
            came = lax.rem(me + size - (k + 1), size)
            pltpu.make_async_remote_copy(
                src_ref=slots.at[came],
                dst_ref=slots.at[came],
                send_sem=send.at[k + 1],
                recv_sem=recv.at[k + 1],
                device_id=peer(lax.rem(me + k + 1, size)),
                device_id_type=MESH,
            ).wait_recv()
        out = slots[0]
        for k in range(1, size):
            out = out + slots[k]
        return out, copies

    gram, first_copies = all_sum(gram, sums, n_lon, lon, lambda i: (lat, i), sum_send, sum_recv)
    gram, last_copies = all_sum(gram, part, n_lat, lat, lambda i: (i, lon), part_send, part_recv)

    work = jnp.where(lane == row + count, 1.0, jnp.where(lane < count, gram, 0.0))
    result = zero
    for k in range(count):
        pivot = work[k : k + 1, :]
        diagonal = pivot[:, k : k + 1]
        pivot = pivot * (1.0 / jnp.sqrt(diagonal))
        result = jnp.where((row == k) & (lane >= k), pivot, result)
        work = work - jnp.where(row > k, (work[:, k : k + 1] * (1.0 / diagonal)), 0.0) * work[k : k + 1, :]
    tile_out[...] = result

    for copy in first_copies + last_copies:
        copy.wait_send()
    for copy in lon_copies:
        copy.wait_send()
    for side in range(2):
        @pl.when(has[side])
        def _():
            for copy in lat_copies[side]:
                copy.wait_send()
    z_copy.wait()


def apply_kernel(scale, inverse, tile, z, basis, factor):
    count, _, rows, width = z.shape
    coefficients = [
        [inverse[p, count + q] * scale for q in range(p + 1)] for p in range(count)
    ]
    for start in range(0, rows, 8):
        values = [z[q, 0, pl.ds(start, 8), :] for q in range(count)]
        for p in range(count):
            total = coefficients[p][0] * values[0]
            for q in range(1, p + 1):
                total = total + coefficients[p][q] * values[q]
            basis[p, 0, pl.ds(start, 8), :] = total

    @pl.when(pl.program_id(0) == 0)
    def _():
        factor[...] = tile[:, :count] * (1.0 / scale)


def body(probes, wind, wind_tend, obs_weight, *, n_lat, n_lon):
    count, levels, rows, width = probes.shape
    entities = count + 5
    packs = (entities + 3) // 4
    tall = rows + 2 * HALO
    f32 = jnp.float32
    z, tile = pl.pallas_call(
        functools.partial(transport_kernel, n_lat, n_lon),
        out_shape=(
            jax.ShapeDtypeStruct(probes.shape, f32),
            jax.ShapeDtypeStruct((8, width), f32),
        ),
        in_specs=[pl.BlockSpec(memory_space=pltpu.HBM)] * 4,
        out_specs=(
            pl.BlockSpec(memory_space=pl.ANY),
            pl.BlockSpec(memory_space=pltpu.VMEM),
        ),
        scratch_shapes=[
            pltpu.VMEM((entities, levels + 2, tall, width), f32),
            pltpu.VMEM((2 * STEPS, count, levels + 2, tall, width), f32),
            pltpu.VMEM((2, 8, width), f32),
            pltpu.VMEM(probes.shape, f32),
            pltpu.VMEM((2, packs, rows, width), f32),
            pltpu.VMEM((2, packs, rows + 2 * HALO, width), f32),
            pltpu.VMEM((n_lon, 8, width), f32),
            pltpu.VMEM((n_lat, 8, width), f32),
            pltpu.SemaphoreType.DMA((4,)),
            pltpu.SemaphoreType.DMA,
            pltpu.SemaphoreType.DMA((2, 4)),
            pltpu.SemaphoreType.DMA((2, 4)),
            pltpu.SemaphoreType.DMA((2, 3)),
            pltpu.SemaphoreType.DMA((2, 3)),
            pltpu.SemaphoreType.DMA((n_lon,)),
            pltpu.SemaphoreType.DMA((n_lon,)),
            pltpu.SemaphoreType.DMA((n_lat,)),
            pltpu.SemaphoreType.DMA((n_lat,)),
        ],
        compiler_params=pltpu.CompilerParams(
            collective_id=0, has_side_effects=True, vmem_limit_bytes=60 * 2**20
        ),
        name="transport",
    )(probes, wind, wind_tend, obs_weight[None])

    cells = levels * rows * width * n_lat * n_lon
    block = pl.BlockSpec((count, 1, rows, width), lambda level: (0, level, 0, 0))
    basis, factor = pl.pallas_call(
        functools.partial(apply_kernel, float(cells) ** 0.5),
        grid=(levels,),
        out_shape=(
            jax.ShapeDtypeStruct(probes.shape, f32),
            jax.ShapeDtypeStruct((count, count), f32),
        ),
        in_specs=[
            pl.BlockSpec(memory_space=pltpu.SMEM),
            pl.BlockSpec((8, width), lambda level: (0, 0)),
            block,
        ],
        out_specs=(block, pl.BlockSpec((count, count), lambda level: (0, 0))),
        compiler_params=pltpu.CompilerParams(vmem_limit_bytes=60 * 2**20),
        name="orthonormal",
    )(tile, tile, z)
    return basis, factor


def solution(mesh):
    placed = (
        P(None, None, "lon", "lat"),
        P(None, None, "lon", "lat"),
        P(None, None, "lon", "lat"),
        P(None, "lon", "lat"),
    )
    return jax.shard_map(
        functools.partial(body, n_lat=mesh.shape["lat"], n_lon=mesh.shape["lon"]),
        mesh=mesh,
        in_specs=placed,
        out_specs=(P(None, None, "lon", "lat"), P()),
        check_vma=False,
    )
```

```python
import functools
import jax
import jax.numpy as jnp
from jax import lax
from jax.experimental import pallas as pl
from jax.experimental.pallas import tpu as pltpu
from jax.sharding import PartitionSpec as P

STEPS = 4
DIFFUSE = 0.24
CENTRE = 1.0 - 4.0 * DIFFUSE
MESH = pl.DeviceIdType.MESH

HALO = 2 * STEPS
WINDOW = 32


def window_shift(side, level, width):
    if side == 0:
        return (WINDOW * level + HALO) % width
    return (WINDOW * level - (width - WINDOW + HALO)) % width


def transport_kernel(
    n_lat, n_lon, probes, wind, tend, weight, z_out, tile_out,
    field, stages, masks, z_buf, send_pack, recv_pack, sums, part,
    load_sem, z_sem, lon_send, lon_recv, lat_send, lat_recv,
    sum_send, sum_recv, part_send, part_recv,
):
    count, levels, rows, width = probes.shape
    entities = count + 5
    lat = lax.axis_index("lat")
    lon = lax.axis_index("lon")
    up_lon, down_lon = lax.rem(lon + 1, n_lon), lax.rem(lon + n_lon - 1, n_lon)
    up_lat, down_lat = lax.rem(lat + 1, n_lat), lax.rem(lat + n_lat - 1, n_lat)
    lane = lax.broadcasted_iota(jnp.int32, (8, width), 1)
    row = lax.broadcasted_iota(jnp.int32, (8, width), 0)
    in_window = lane % WINDOW

    barrier = pltpu.get_barrier_semaphore()

    def greet(to_lat, to_lon):
        pl.semaphore_signal(barrier, inc=1, device_id=(to_lat, to_lon), device_id_type=MESH)

    for k in range(1, n_lon):
        greet(lat, lax.rem(lon + k, n_lon))
    for k in range(1, n_lat):
        greet(lax.rem(lat + k, n_lat), lon)
    for to_lat in (up_lat, down_lat):
        for to_lon in (up_lon, down_lon):
            greet(to_lat, to_lon)

    placed = ((probes, 0, count), (wind, count, 2), (tend, count + 2, 2), (weight, count + 4, 1))
    loads = [
        pltpu.make_async_copy(
            source,
            field.at[pl.ds(first, size), pl.ds(0, levels), pl.ds(HALO, rows), :],
            load_sem.at[k],
        )
        for k, (source, first, size) in enumerate(placed)
    ]
    for load in loads:
        load.start()

    zero = jnp.zeros((8, width), jnp.float32)
    total = width * n_lat
    for side, first in ((0, -HALO), (1, width - WINDOW + HALO)):
        column = lat * width + first + in_window
        masks[side] = jnp.where((column >= 0) & (column < total), 1.0, 0.0)

    pl.semaphore_wait(barrier, n_lon + n_lat + 2)

    lon_copies = []
    for d, (to_lon, src_row, dst_row) in enumerate(
        ((up_lon, rows - HALO, 0), (down_lon, 0, HALO + rows))
    ):
        for k, (source, first, size) in enumerate(placed):
            copy = pltpu.make_async_remote_copy(
                src_ref=source.at[:, :, pl.ds(src_row, HALO), :],
                dst_ref=field.at[pl.ds(first, size), pl.ds(0, levels), pl.ds(dst_row, HALO), :],
                send_sem=lon_send.at[d, k],
                recv_sem=lon_recv.at[d, k],
                device_id=(lat, to_lon),
                device_id_type=MESH,
            )
            copy.start()
            lon_copies.append(copy)

    def own_window(entity, side, start):
        made = None
        for level in range(levels):
            piece = pltpu.roll(
                field[entity, level, pl.ds(start, 8), :], window_shift(side, level, width), 1
            )
            made = piece if made is None else jnp.where(lane >= WINDOW * level, piece, made)
        return made

    for load in loads:
        load.wait()

    def pack(group, carry):
        start = pl.multiple_of(HALO + 8 * group, 8)
        to = pl.multiple_of(8 * group, 8)
        for side in range(2):
            packed = [zero] * ((entities + 3) // 4)
            for entity in range(entities):
                made = own_window(entity, side, start)
                field[entity, levels + side, pl.ds(start, 8), :] = made
                slot = entity % 4
                moved = pltpu.roll(made, (8 * slot - (8 if side == 0 else 16)) % width, 1)
                packed[entity // 4] = jnp.where(
                    in_window // 8 == slot, moved, packed[entity // 4]
                )
            for k, value in enumerate(packed):
                send_pack[side, k, pl.ds(to, 8), :] = value
        return carry

    lax.fori_loop(0, rows // 8, pack, 0, unroll=2)

    has = (lat > 0, lat < n_lat - 1)
    lat_copies = ([], [])
    for side, to_lat in ((0, down_lat), (1, up_lat)):
        for k, (to_lon, src_row, size, dst_row) in enumerate(
            (
                (lon, 0, rows, HALO),
                (up_lon, rows - HALO, HALO, 0),
                (down_lon, 0, HALO, HALO + rows),
            )
        ):
            lat_copies[side].append(
                pltpu.make_async_remote_copy(
                    src_ref=send_pack.at[side, :, pl.ds(src_row, size), :],
                    dst_ref=recv_pack.at[1 - side, :, pl.ds(dst_row, size), :],
                    send_sem=lat_send.at[side, k],
                    recv_sem=lat_recv.at[side, k],
                    device_id=(to_lat, to_lon),
                    device_id_type=MESH,
                )
            )

    for side in range(2):
        @pl.when(has[side])
        def _():
            for copy in lat_copies[side]:
                copy.start()

    groups = rows // 8 + 2
    buffers = [field] + [stages.at[k] for k in range(2 * STEPS)]

    def above(ref, lead, start, closed):
        if closed:
            return pltpu.roll(ref[(*lead, pl.ds(start, 8), slice(None))], 1, 0)
        return ref[(*lead, pl.ds(start - 1, 8), slice(None))]

    def below(ref, lead, start, closed):
        if closed:
            return pltpu.roll(ref[(*lead, pl.ds(start, 8), slice(None))], 7, 0)
        return ref[(*lead, pl.ds(start + 1, 8), slice(None))]

    def same(ref, lead, start, closed):
        return ref[(*lead, pl.ds(start, 8), slice(None))]

    def rate(which, step, level, start, read=same, closed=False):
        now = read(field, (count + which, level), start, closed)
        if step:
            now = now + step * read(field, (count + 2 + which, level), start, closed)
        return 0.5 * now

    def run_step(number, first_level, last_level, chosen, top, bottom, unroll):
        source, target = buffers[number], buffers[number + 1]
        adjoint = number >= STEPS
        step = 2 * STEPS - 1 - number if adjoint else number

        def body(level, carry):
            for group in chosen:
                start = 8 * group
                if adjoint:
                    north = rate(1, step, level, start)
                    before = DIFFUSE - rate(0, step, level, start, above, group == top)
                    after = DIFFUSE + rate(0, step, level, start, below, group == bottom)
                    left = pltpu.roll(DIFFUSE - north, 1, 1)
                    right = pltpu.roll(DIFFUSE + north, width - 1, 1)
                else:
                    east = rate(0, step, level, start)
                    north = rate(1, step, level, start)
                    after = DIFFUSE - east
                    before = DIFFUSE + east
                    right = DIFFUSE - north
                    left = DIFFUSE + north
                centre = CENTRE
                scale = None
                if first_level >= levels:
                    scale = masks[level - levels]
                if number == STEPS - 1:
                    seen = field[count + 4, level, pl.ds(start, 8), :]
                    scale = seen if scale is None else scale * seen
                if scale is not None:
                    centre, before, after, left, right = (
                        scale * x for x in (centre, before, after, left, right)
                    )
                for probe in range(count):
                    lead = (probe, level)
                    middle = source[probe, level, pl.ds(start, 8), :]
                    target[probe, level, pl.ds(start, 8), :] = (
                        (centre * middle + after * below(source, lead, start, group == bottom))
                        + (before * above(source, lead, start, group == top)
                           + right * pltpu.roll(middle, width - 1, 1))
                        + left * pltpu.roll(middle, 1, 1)
                    )
            return carry

        lax.fori_loop(first_level, last_level, body, 0, unroll=unroll)

    for number in range(2 * STEPS):
        run_step(number, 0, levels, range(1, groups - 1), 1, groups - 2, 2)

    for copy in lon_copies:
        copy.wait_recv()

    for start in (0, HALO + rows):
        for entity in range(entities):
            for side in range(2):
                field[entity, levels + side, pl.ds(start, 8), :] = own_window(entity, side, start)

    for side in range(2):
        @pl.when(has[side])
        def _():
            for copy in lat_copies[1 - side]:
                copy.wait_recv()

        @pl.when(jnp.logical_not(has[side]))
        def _():
            recv_pack[side] = jnp.zeros(recv_pack.shape[1:], jnp.float32)

    def unpack(group, carry):
        at = pl.multiple_of(8 * group, 8)
        for side in range(2):
            here = in_window < 8 if side == 0 else in_window >= 24
            for entity in range(entities):
                slot = entity % 4
                got = recv_pack[side, entity // 4, pl.ds(at, 8), :]
                moved = pltpu.roll(got, ((0 if side == 0 else 24) - 8 * slot) % width, 1)
                held = field[entity, levels + side, pl.ds(at, 8), :]
                field[entity, levels + side, pl.ds(at, 8), :] = jnp.where(here, moved, held)
        return carry

    lax.fori_loop(0, groups, unpack, 0, unroll=5)

    for number in range(2 * STEPS):
        last = int(number == 2 * STEPS - 1)
        outer = (1, groups - 2) if last else (0, 1, groups - 2, groups - 1)
        run_step(number, 0, levels, outer, 0, groups - 1, levels)
        run_step(number, levels, levels + 2, range(last, groups - last), 0, groups - 1, 2)
    source = buffers[-1]

    pairs = [(p, q) for p in range(count) for q in range(p, count)]

    accs = [zero] * len(pairs)
    for level in range(levels):
        def gather(group, accs):
            start = pl.multiple_of(HALO + 8 * group, 8)
            to = pl.multiple_of(8 * group, 8)
            values = []
            for probe in range(count):
                first = pltpu.roll(
                    source[probe, levels, pl.ds(start, 8), :],
                    (width - window_shift(0, level, width)) % width, 1,
                )
                last = pltpu.roll(
                    source[probe, levels + 1, pl.ds(start, 8), :],
                    (width - window_shift(1, level, width)) % width, 1,
                )
                value = source[probe, level, pl.ds(start, 8), :]
                value = jnp.where(lane < HALO, first, value)
                value = jnp.where(lane >= width - HALO, last, value)
                z_buf[probe, level, pl.ds(to, 8), :] = value
                values.append(value)
            return tuple(a + values[p] * values[q] for a, (p, q) in zip(accs, pairs))

        accs = lax.fori_loop(0, rows // 8, gather, tuple(accs), unroll=4)

    z_copy = pltpu.make_async_copy(z_buf, z_out, z_sem)
    z_copy.start()

    reduced = {
        pair: jnp.broadcast_to(jnp.sum(acc, axis=0, keepdims=True), (8, width))
        for pair, acc in zip(pairs, accs)
    }
    gram = zero
    for q in range(count):
        column = zero
        for p in range(count):
            column = jnp.where(row == p, reduced[(min(p, q), max(p, q))], column)
        gram = jnp.where(lane == q, jnp.sum(column, axis=1, keepdims=True), gram)

    def all_sum(value, slots, size, me, peer, send, recv):
        slots[me] = value
        copies = []
        for k in range(1, size):
            copy = pltpu.make_async_remote_copy(
                src_ref=slots.at[me],
                dst_ref=slots.at[me],
                send_sem=send.at[k],
                recv_sem=recv.at[k],
                device_id=peer(lax.rem(me + k, size)),
                device_id_type=MESH,
            )
            copy.start()
            copies.append(copy)
        for k, copy in enumerate(copies):
            came = lax.rem(me + size - (k + 1), size)
            pltpu.make_async_remote_copy(
                src_ref=slots.at[came],
                dst_ref=slots.at[came],
                send_sem=send.at[k + 1],
                recv_sem=recv.at[k + 1],
                device_id=peer(lax.rem(me + k + 1, size)),
                device_id_type=MESH,
            ).wait_recv()
        out = slots[0]
        for k in range(1, size):
            out = out + slots[k]
        return out, copies

    gram, first_copies = all_sum(gram, sums, n_lon, lon, lambda i: (lat, i), sum_send, sum_recv)
    gram, last_copies = all_sum(gram, part, n_lat, lat, lambda i: (i, lon), part_send, part_recv)

    work = jnp.where(lane == row + count, 1.0, jnp.where(lane < count, gram, 0.0))
    result = zero
    for k in range(count):
        pivot = work[k : k + 1, :]
        diagonal = pivot[:, k : k + 1]
        pivot = pivot * (1.0 / jnp.sqrt(diagonal))
        result = jnp.where((row == k) & (lane >= k), pivot, result)
        work = work - jnp.where(row > k, (work[:, k : k + 1] * (1.0 / diagonal)), 0.0) * work[k : k + 1, :]
    tile_out[...] = result

    for copy in first_copies + last_copies:
        copy.wait_send()
    for copy in lon_copies:
        copy.wait_send()
    for side in range(2):
        @pl.when(has[side])
        def _():
            for copy in lat_copies[side]:
                copy.wait_send()
    z_copy.wait()


def apply_kernel(scale, tile, z, basis, factor, tile_buf, z_buf, out_buf, tile_sem, in_sem, out_sem):
    count, levels, rows, width = z.shape
    first = pltpu.make_async_copy(tile, tile_buf, tile_sem)
    first.start()
    loads = [
        pltpu.make_async_copy(z.at[:, level], z_buf.at[:, level], in_sem.at[level])
        for level in range(levels)
    ]
    for load in loads:
        load.start()
    first.wait()
    found = tile_buf[...]
    factor[...] = found[:, :count] * (1.0 / scale)
    found = found * scale
    coefficients = [
        [
            jnp.broadcast_to(found[p : p + 1, count + q : count + q + 1], (8, width))
            for q in range(p + 1)
        ]
        for p in range(count)
    ]
    stores = []
    for level in range(levels):
        loads[level].wait()
        for start in range(0, rows, 8):
            values = [z_buf[q, level, pl.ds(start, 8), :] for q in range(count)]
            for p in range(count):
                total = coefficients[p][0] * values[0]
                for q in range(1, p + 1):
                    total = total + coefficients[p][q] * values[q]
                out_buf[p, level, pl.ds(start, 8), :] = total
        store = pltpu.make_async_copy(out_buf.at[:, level], basis.at[:, level], out_sem.at[level])
        store.start()
        stores.append(store)
    for store in stores:
        store.wait()


def body(probes, wind, wind_tend, obs_weight, *, n_lat, n_lon):
    count, levels, rows, width = probes.shape
    entities = count + 5
    packs = (entities + 3) // 4
    tall = rows + 2 * HALO
    f32 = jnp.float32
    z, tile = pl.pallas_call(
        functools.partial(transport_kernel, n_lat, n_lon),
        out_shape=(
            jax.ShapeDtypeStruct(probes.shape, f32),
            jax.ShapeDtypeStruct((8, width), f32),
        ),
        in_specs=[pl.BlockSpec(memory_space=pltpu.HBM)] * 4,
        out_specs=(
            pl.BlockSpec(memory_space=pl.ANY),
            pl.BlockSpec(memory_space=pltpu.VMEM),
        ),
        scratch_shapes=[
            pltpu.VMEM((entities, levels + 2, tall, width), f32),
            pltpu.VMEM((2 * STEPS, count, levels + 2, tall, width), f32),
            pltpu.VMEM((2, 8, width), f32),
            pltpu.VMEM(probes.shape, f32),
            pltpu.VMEM((2, packs, rows, width), f32),
            pltpu.VMEM((2, packs, rows + 2 * HALO, width), f32),
            pltpu.VMEM((n_lon, 8, width), f32),
            pltpu.VMEM((n_lat, 8, width), f32),
            pltpu.SemaphoreType.DMA((4,)),
            pltpu.SemaphoreType.DMA,
            pltpu.SemaphoreType.DMA((2, 4)),
            pltpu.SemaphoreType.DMA((2, 4)),
            pltpu.SemaphoreType.DMA((2, 3)),
            pltpu.SemaphoreType.DMA((2, 3)),
            pltpu.SemaphoreType.DMA((n_lon,)),
            pltpu.SemaphoreType.DMA((n_lon,)),
            pltpu.SemaphoreType.DMA((n_lat,)),
            pltpu.SemaphoreType.DMA((n_lat,)),
        ],
        compiler_params=pltpu.CompilerParams(
            collective_id=0, has_side_effects=True, vmem_limit_bytes=60 * 2**20
        ),
        name="transport",
    )(probes, wind, wind_tend, obs_weight[None])

    cells = levels * rows * width * n_lat * n_lon
    basis, factor = pl.pallas_call(
        functools.partial(apply_kernel, float(cells) ** 0.5),
        out_shape=(
            jax.ShapeDtypeStruct(probes.shape, f32),
            jax.ShapeDtypeStruct((count, count), f32),
        ),
        in_specs=[pl.BlockSpec(memory_space=pltpu.HBM)] * 2,
        out_specs=(
            pl.BlockSpec(memory_space=pltpu.HBM),
            pl.BlockSpec(memory_space=pltpu.VMEM),
        ),
        scratch_shapes=[
            pltpu.VMEM((8, width), f32),
            pltpu.VMEM(probes.shape, f32),
            pltpu.VMEM(probes.shape, f32),
            pltpu.SemaphoreType.DMA,
            pltpu.SemaphoreType.DMA((levels,)),
            pltpu.SemaphoreType.DMA((levels,)),
        ],
        compiler_params=pltpu.CompilerParams(vmem_limit_bytes=60 * 2**20),
        name="orthonormal",
    )(tile, z)
    return basis, factor


def solution(mesh):
    placed = (
        P(None, None, "lon", "lat"),
        P(None, None, "lon", "lat"),
        P(None, None, "lon", "lat"),
        P(None, "lon", "lat"),
    )
    return jax.shard_map(
        functools.partial(body, n_lat=mesh.shape["lat"], n_lon=mesh.shape["lon"]),
        mesh=mesh,
        in_specs=placed,
        out_specs=(P(None, None, "lon", "lat"), P()),
        check_vma=False,
    )
```

```python
import functools
import jax
import jax.numpy as jnp
from jax import lax
from jax.experimental import pallas as pl
from jax.experimental.pallas import tpu as pltpu
from jax.sharding import PartitionSpec as P

STEPS = 4
DIFFUSE = 0.24
CENTRE = 1.0 - 4.0 * DIFFUSE
MESH = pl.DeviceIdType.MESH

HALO = 2 * STEPS
WINDOW = 32


def window_shift(side, level, width):
    if side == 0:
        return (WINDOW * level + HALO) % width
    return (WINDOW * level - (width - WINDOW + HALO)) % width


def transport_kernel(
    n_lat, n_lon, probes, wind, tend, weight, z_out, tile_out,
    field, stages, masks, z_buf, send_pack, recv_pack, sums, part,
    load_sem, z_sem, lon_send, lon_recv, lat_send, lat_recv,
    sum_send, sum_recv, part_send, part_recv,
):
    count, levels, rows, width = probes.shape
    entities = count + 5
    lat = lax.axis_index("lat")
    lon = lax.axis_index("lon")
    up_lon, down_lon = lax.rem(lon + 1, n_lon), lax.rem(lon + n_lon - 1, n_lon)
    up_lat, down_lat = lax.rem(lat + 1, n_lat), lax.rem(lat + n_lat - 1, n_lat)
    lane = lax.broadcasted_iota(jnp.int32, (8, width), 1)
    row = lax.broadcasted_iota(jnp.int32, (8, width), 0)
    in_window = lane % WINDOW

    barrier = pltpu.get_barrier_semaphore()

    def greet(to_lat, to_lon):
        pl.semaphore_signal(barrier, inc=1, device_id=(to_lat, to_lon), device_id_type=MESH)

    for k in range(1, n_lon):
        greet(lat, lax.rem(lon + k, n_lon))
    for k in range(1, n_lat):
        greet(lax.rem(lat + k, n_lat), lon)
    for to_lat in (up_lat, down_lat):
        for to_lon in (up_lon, down_lon):
            greet(to_lat, to_lon)

    placed = ((probes, 0, count), (wind, count, 2), (tend, count + 2, 2), (weight, count + 4, 1))
    loads = [
        pltpu.make_async_copy(
            source,
            field.at[pl.ds(first, size), pl.ds(0, levels), pl.ds(HALO, rows), :],
            load_sem.at[k],
        )
        for k, (source, first, size) in enumerate(placed)
    ]
    for load in loads:
        load.start()

    zero = jnp.zeros((8, width), jnp.float32)
    total = width * n_lat
    for side, first in ((0, -HALO), (1, width - WINDOW + HALO)):
        column = lat * width + first + in_window
        masks[side] = jnp.where((column >= 0) & (column < total), 1.0, 0.0)

    pl.semaphore_wait(barrier, n_lon + n_lat + 2)

    lon_copies = []
    for d, (to_lon, src_row, dst_row) in enumerate(
        ((up_lon, rows - HALO, 0), (down_lon, 0, HALO + rows))
    ):
        for k, (source, first, size) in enumerate(placed):
            copy = pltpu.make_async_remote_copy(
                src_ref=source.at[:, :, pl.ds(src_row, HALO), :],
                dst_ref=field.at[pl.ds(first, size), pl.ds(0, levels), pl.ds(dst_row, HALO), :],
                send_sem=lon_send.at[d, k],
                recv_sem=lon_recv.at[d, k],
                device_id=(lat, to_lon),
                device_id_type=MESH,
            )
            copy.start()
            lon_copies.append(copy)

    def own_window(entity, side, start):
        made = None
        for level in range(levels):
            piece = pltpu.roll(
                field[entity, level, pl.ds(start, 8), :], window_shift(side, level, width), 1
            )
            made = piece if made is None else jnp.where(lane >= WINDOW * level, piece, made)
        return made

    for load in loads:
        load.wait()

    def pack(group, carry):
        start = pl.multiple_of(HALO + 8 * group, 8)
        to = pl.multiple_of(8 * group, 8)
        for side in range(2):
            packed = [zero] * ((entities + 3) // 4)
            for entity in range(entities):
                made = own_window(entity, side, start)
                field[entity, levels + side, pl.ds(start, 8), :] = made
                slot = entity % 4
                moved = pltpu.roll(made, (8 * slot - (8 if side == 0 else 16)) % width, 1)
                packed[entity // 4] = jnp.where(
                    in_window // 8 == slot, moved, packed[entity // 4]
                )
            for k, value in enumerate(packed):
                send_pack[side, k, pl.ds(to, 8), :] = value
        return carry

    lax.fori_loop(0, rows // 8, pack, 0)

    has = (lat > 0, lat < n_lat - 1)
    lat_copies = ([], [])
    for side, to_lat in ((0, down_lat), (1, up_lat)):
        for k, (to_lon, src_row, size, dst_row) in enumerate(
            (
                (lon, 0, rows, HALO),
                (up_lon, rows - HALO, HALO, 0),
                (down_lon, 0, HALO, HALO + rows),
            )
        ):
            lat_copies[side].append(
                pltpu.make_async_remote_copy(
                    src_ref=send_pack.at[side, :, pl.ds(src_row, size), :],
                    dst_ref=recv_pack.at[1 - side, :, pl.ds(dst_row, size), :],
                    send_sem=lat_send.at[side, k],
                    recv_sem=lat_recv.at[side, k],
                    device_id=(to_lat, to_lon),
                    device_id_type=MESH,
                )
            )

    for side in range(2):
        @pl.when(has[side])
        def _():
            for copy in lat_copies[side]:
                copy.start()

    groups = rows // 8 + 2
    buffers = [field] + [stages.at[k] for k in range(2 * STEPS)]

    def above(ref, lead, start, closed):
        if closed:
            return pltpu.roll(ref[(*lead, pl.ds(start, 8), slice(None))], 1, 0)
        return ref[(*lead, pl.ds(start - 1, 8), slice(None))]

    def below(ref, lead, start, closed):
        if closed:
            return pltpu.roll(ref[(*lead, pl.ds(start, 8), slice(None))], 7, 0)
        return ref[(*lead, pl.ds(start + 1, 8), slice(None))]

    def same(ref, lead, start, closed):
        return ref[(*lead, pl.ds(start, 8), slice(None))]

    def rate(which, step, level, start, read=same, closed=False):
        now = read(field, (count + which, level), start, closed)
        if step:
            now = now + step * read(field, (count + 2 + which, level), start, closed)
        return 0.5 * now

    def run_step(number, first_level, last_level, chosen, top, bottom, unroll):
        source, target = buffers[number], buffers[number + 1]
        adjoint = number >= STEPS
        step = 2 * STEPS - 1 - number if adjoint else number

        def body(level, carry):
            for group in chosen:
                start = 8 * group
                if adjoint:
                    north = rate(1, step, level, start)
                    before = DIFFUSE - rate(0, step, level, start, above, group == top)
                    after = DIFFUSE + rate(0, step, level, start, below, group == bottom)
                    left = pltpu.roll(DIFFUSE - north, 1, 1)
                    right = pltpu.roll(DIFFUSE + north, width - 1, 1)
                else:
                    east = rate(0, step, level, start)
                    north = rate(1, step, level, start)
                    after = DIFFUSE - east
                    before = DIFFUSE + east
                    right = DIFFUSE - north
                    left = DIFFUSE + north
                centre = CENTRE
                scale = None
                if first_level >= levels:
                    scale = masks[level - levels]
                if number == STEPS - 1:
                    seen = field[count + 4, level, pl.ds(start, 8), :]
                    scale = seen if scale is None else scale * seen
                if scale is not None:
                    centre, before, after, left, right = (
                        scale * x for x in (centre, before, after, left, right)
                    )
                for probe in range(count):
                    lead = (probe, level)
                    middle = source[probe, level, pl.ds(start, 8), :]
                    target[probe, level, pl.ds(start, 8), :] = (
                        (centre * middle + after * below(source, lead, start, group == bottom))
                        + (before * above(source, lead, start, group == top)
                           + right * pltpu.roll(middle, width - 1, 1))
                        + left * pltpu.roll(middle, 1, 1)
                    )
            return carry

        lax.fori_loop(first_level, last_level, body, 0, unroll=unroll)

    for number in range(2 * STEPS):
        run_step(number, 0, levels, range(1, groups - 1), 1, groups - 2, 1)

    for copy in lon_copies:
        copy.wait_recv()

    for start in (0, HALO + rows):
        for entity in range(entities):
            for side in range(2):
                field[entity, levels + side, pl.ds(start, 8), :] = own_window(entity, side, start)

    for side in range(2):
        @pl.when(has[side])
        def _():
            for copy in lat_copies[1 - side]:
                copy.wait_recv()

        @pl.when(jnp.logical_not(has[side]))
        def _():
            recv_pack[side] = jnp.zeros(recv_pack.shape[1:], jnp.float32)

    def unpack(group, carry):
        at = pl.multiple_of(8 * group, 8)
        for side in range(2):
            here = in_window < 8 if side == 0 else in_window >= 24
            for entity in range(entities):
                slot = entity % 4
                got = recv_pack[side, entity // 4, pl.ds(at, 8), :]
                moved = pltpu.roll(got, ((0 if side == 0 else 24) - 8 * slot) % width, 1)
                held = field[entity, levels + side, pl.ds(at, 8), :]
                field[entity, levels + side, pl.ds(at, 8), :] = jnp.where(here, moved, held)
        return carry

    lax.fori_loop(0, groups, unpack, 0, unroll=2)

    for number in range(2 * STEPS):
        last = int(number == 2 * STEPS - 1)
        outer = (1, groups - 2) if last else (0, 1, groups - 2, groups - 1)
        run_step(number, 0, levels, outer, 0, groups - 1, 2)
        run_step(number, levels, levels + 2, range(last, groups - last), 0, groups - 1, 1)
    source = buffers[-1]

    pairs = [(p, q) for p in range(count) for q in range(p, count)]

    accs = [zero] * len(pairs)
    for level in range(levels):
        def gather(group, accs):
            start = pl.multiple_of(HALO + 8 * group, 8)
            to = pl.multiple_of(8 * group, 8)
            values = []
            for probe in range(count):
                first = pltpu.roll(
                    source[probe, levels, pl.ds(start, 8), :],
                    (width - window_shift(0, level, width)) % width, 1,
                )
                last = pltpu.roll(
                    source[probe, levels + 1, pl.ds(start, 8), :],
                    (width - window_shift(1, level, width)) % width, 1,
                )
                value = source[probe, level, pl.ds(start, 8), :]
                value = jnp.where(lane < HALO, first, value)
                value = jnp.where(lane >= width - HALO, last, value)
                z_buf[probe, level, pl.ds(to, 8), :] = value
                values.append(value)
            return tuple(a + values[p] * values[q] for a, (p, q) in zip(accs, pairs))

        accs = lax.fori_loop(0, rows // 8, gather, tuple(accs), unroll=4)

    z_copy = pltpu.make_async_copy(z_buf, z_out, z_sem)
    z_copy.start()

    reduced = {
        pair: jnp.broadcast_to(jnp.sum(acc, axis=0, keepdims=True), (8, width))
        for pair, acc in zip(pairs, accs)
    }
    gram = zero
    for q in range(count):
        column = zero
        for p in range(count):
            column = jnp.where(row == p, reduced[(min(p, q), max(p, q))], column)
        gram = jnp.where(lane == q, jnp.sum(column, axis=1, keepdims=True), gram)

    def all_sum(value, slots, size, me, peer, send, recv):
        slots[me] = value
        copies = []
        for k in range(1, size):
            copy = pltpu.make_async_remote_copy(
                src_ref=slots.at[me],
                dst_ref=slots.at[me],
                send_sem=send.at[k],
                recv_sem=recv.at[k],
                device_id=peer(lax.rem(me + k, size)),
                device_id_type=MESH,
            )
            copy.start()
            copies.append(copy)
        for k, copy in enumerate(copies):
            came = lax.rem(me + size - (k + 1), size)
            pltpu.make_async_remote_copy(
                src_ref=slots.at[came],
                dst_ref=slots.at[came],
                send_sem=send.at[k + 1],
                recv_sem=recv.at[k + 1],
                device_id=peer(lax.rem(me + k + 1, size)),
                device_id_type=MESH,
            ).wait_recv()
        out = slots[0]
        for k in range(1, size):
            out = out + slots[k]
        return out, copies

    gram, first_copies = all_sum(gram, sums, n_lon, lon, lambda i: (lat, i), sum_send, sum_recv)
    gram, last_copies = all_sum(gram, part, n_lat, lat, lambda i: (i, lon), part_send, part_recv)

    work = jnp.where(lane == row + count, 1.0, jnp.where(lane < count, gram, 0.0))
    result = zero
    for k in range(count):
        pivot = work[k : k + 1, :]
        diagonal = pivot[:, k : k + 1]
        pivot = pivot * (1.0 / jnp.sqrt(diagonal))
        result = jnp.where((row == k) & (lane >= k), pivot, result)
        work = work - jnp.where(row > k, (work[:, k : k + 1] * (1.0 / diagonal)), 0.0) * work[k : k + 1, :]
    tile_out[...] = result

    for copy in first_copies + last_copies:
        copy.wait_send()
    for copy in lon_copies:
        copy.wait_send()
    for side in range(2):
        @pl.when(has[side])
        def _():
            for copy in lat_copies[side]:
                copy.wait_send()
    z_copy.wait()


def apply_kernel(scale, tile, z, basis, factor, tile_buf, z_buf, out_buf, tile_sem, in_sem, out_sem):
    count, levels, rows, width = z.shape
    first = pltpu.make_async_copy(tile, tile_buf, tile_sem)
    first.start()
    loads = [
        pltpu.make_async_copy(z.at[:, level], z_buf.at[:, level], in_sem.at[level])
        for level in range(levels)
    ]
    for load in loads:
        load.start()
    first.wait()
    found = tile_buf[...]
    factor[...] = found[:, :count] * (1.0 / scale)
    found = found * scale
    coefficients = [
        [
            jnp.broadcast_to(found[p : p + 1, count + q : count + q + 1], (8, width))
            for q in range(p + 1)
        ]
        for p in range(count)
    ]
    stores = []
    for level in range(levels):
        loads[level].wait()
        for start in range(0, rows, 8):
            values = [z_buf[q, level, pl.ds(start, 8), :] for q in range(count)]
            for p in range(count):
                total = coefficients[p][0] * values[0]
                for q in range(1, p + 1):
                    total = total + coefficients[p][q] * values[q]
                out_buf[p, level, pl.ds(start, 8), :] = total
        store = pltpu.make_async_copy(out_buf.at[:, level], basis.at[:, level], out_sem.at[level])
        store.start()
        stores.append(store)
    for store in stores:
        store.wait()


def body(probes, wind, wind_tend, obs_weight, *, n_lat, n_lon):
    count, levels, rows, width = probes.shape
    entities = count + 5
    packs = (entities + 3) // 4
    tall = rows + 2 * HALO
    f32 = jnp.float32
    z, tile = pl.pallas_call(
        functools.partial(transport_kernel, n_lat, n_lon),
        out_shape=(
            jax.ShapeDtypeStruct(probes.shape, f32),
            jax.ShapeDtypeStruct((8, width), f32),
        ),
        in_specs=[pl.BlockSpec(memory_space=pltpu.HBM)] * 4,
        out_specs=(
            pl.BlockSpec(memory_space=pl.ANY),
            pl.BlockSpec(memory_space=pltpu.VMEM),
        ),
        scratch_shapes=[
            pltpu.VMEM((entities, levels + 2, tall, width), f32),
            pltpu.VMEM((2 * STEPS, count, levels + 2, tall, width), f32),
            pltpu.VMEM((2, 8, width), f32),
            pltpu.VMEM(probes.shape, f32),
            pltpu.VMEM((2, packs, rows, width), f32),
            pltpu.VMEM((2, packs, rows + 2 * HALO, width), f32),
            pltpu.VMEM((n_lon, 8, width), f32),
            pltpu.VMEM((n_lat, 8, width), f32),
            pltpu.SemaphoreType.DMA((4,)),
            pltpu.SemaphoreType.DMA,
            pltpu.SemaphoreType.DMA((2, 4)),
            pltpu.SemaphoreType.DMA((2, 4)),
            pltpu.SemaphoreType.DMA((2, 3)),
            pltpu.SemaphoreType.DMA((2, 3)),
            pltpu.SemaphoreType.DMA((n_lon,)),
            pltpu.SemaphoreType.DMA((n_lon,)),
            pltpu.SemaphoreType.DMA((n_lat,)),
            pltpu.SemaphoreType.DMA((n_lat,)),
        ],
        compiler_params=pltpu.CompilerParams(
            collective_id=0, has_side_effects=True, vmem_limit_bytes=60 * 2**20
        ),
        name="transport",
    )(probes, wind, wind_tend, obs_weight[None])

    cells = levels * rows * width * n_lat * n_lon
    basis, factor = pl.pallas_call(
        functools.partial(apply_kernel, float(cells) ** 0.5),
        out_shape=(
            jax.ShapeDtypeStruct(probes.shape, f32),
            jax.ShapeDtypeStruct((count, count), f32),
        ),
        in_specs=[pl.BlockSpec(memory_space=pltpu.HBM)] * 2,
        out_specs=(
            pl.BlockSpec(memory_space=pltpu.HBM),
            pl.BlockSpec(memory_space=pltpu.VMEM),
        ),
        scratch_shapes=[
            pltpu.VMEM((8, width), f32),
            pltpu.VMEM(probes.shape, f32),
            pltpu.VMEM(probes.shape, f32),
            pltpu.SemaphoreType.DMA,
            pltpu.SemaphoreType.DMA((levels,)),
            pltpu.SemaphoreType.DMA((levels,)),
        ],
        compiler_params=pltpu.CompilerParams(vmem_limit_bytes=60 * 2**20),
        name="orthonormal",
    )(tile, z)
    return basis, factor


def solution(mesh):
    placed = (
        P(None, None, "lon", "lat"),
        P(None, None, "lon", "lat"),
        P(None, None, "lon", "lat"),
        P(None, "lon", "lat"),
    )
    return jax.shard_map(
        functools.partial(body, n_lat=mesh.shape["lat"], n_lon=mesh.shape["lon"]),
        mesh=mesh,
        in_specs=placed,
        out_specs=(P(None, None, "lon", "lat"), P()),
        check_vma=False,
    )
```
